32 devices in a mesh: space: 16 (over z, y, x), blk: 2 (over core).
Axes of the slice: x: 2, y: 2, z: 4, core: 2. Of those that a mesh axis runs over, the one named last changes fastest.
Arguments:
- coords: float32 [32, 2, 256], P(('space', 'blk'))
- values: float32 [32, 32, 256], P(('space', 'blk')), may hold values from -6 to 6
- valid: int32 [32], P(('space', 'blk')), may hold values from 128 to 256, as said below
- neighbours: int32 [32, 3], P(('space', 'blk')), may hold values from -1 to 30, as said below
- grid: float32 [32, 2, 256], P(('space', 'blk'))
- sources: int32 [32, 3], P(('space', 'blk')), may hold values from -1 to 31, as said below
- theta: float32 [6], replicated, may hold values from 0.05 to 1.6
Outputs:
- whitened: float32 [32, 32, 256], P(('space', 'blk'))
- predicted: float32 [32, 32, 256], P(('space', 'blk'))
- loglik: float32 [], replicated
The draws below stay inside these ranges and needn't reach their ends.
Inputs may be any that keep to these rules, and one draw needn't show every extreme that they name: `neighbours`: a row lists distinct earlier blocks b - o with 1 <= o <= 4, always including b - 1, entries below 0 given as -1. `sources`: tile t lists distinct blocks e - o with 0 <= o < 4, always including e, e the last block of the device holding tile t, entries below 0 given as -1. `valid`: every even-numbered block is full.
All inputs are finite; a program needn't handle non-finite values.
Results may differ from the reference program's by a relative error of at most 0.0003.
Values sent between devices are 32-bit elements; how exact they have to be, the bound alone decides.
No kernel may reach another device: no remote copies, remote signals or barrier semaphores. Data moves between devices by JAX's collectives and lax.ppermute only.
A program may use at most 128 MiB of HBM per device.

```python
import math
import jax
import jax.numpy as jnp
from jax import lax

NB = 1
TP = 1
BS = 256
PS = 256
R = 32
K = 3
KP = 3
NEWTON = 8
WINDOW = 4
BLOCKS = 32
TILES = 32


def draw_coords(key, part):
    key = jax.random.fold_in(key, 11)
    jitter = jax.random.uniform(key, (BLOCKS, 2, BS), jnp.float32, -2.0, 2.0)
    centre = jnp.arange(BLOCKS).astype(jnp.float32) / WINDOW
    offset = jnp.stack([centre, jnp.zeros_like(centre)], axis=1)[:, :, None]
    return jitter + offset


def draw_grid(key, part):
    key = jax.random.fold_in(key, 23)
    jitter = jax.random.uniform(key, (TILES, 2, PS), jnp.float32, -2.0, 2.0)
    centre = jnp.arange(TILES).astype(jnp.float32) * NB / (TP * WINDOW)
    offset = jnp.stack([centre, jnp.zeros_like(centre)], axis=1)[:, :, None]
    return jitter + offset


def draw_valid(key, part):
    key = jax.random.fold_in(key, 37)
    counts = jax.random.randint(key, (BLOCKS,), BS // 2, BS + 1)
    full = jnp.arange(BLOCKS) % 2 == 0
    return jnp.where(full, BS, counts).astype(jnp.int32)


def draw_neighbours(key, part):
    key = jax.random.fold_in(key, 41)
    scores = jax.random.randint(key, (BLOCKS, WINDOW), 0, 1 << 20) * WINDOW + jnp.arange(WINDOW)[None, :]
    forced = jnp.where(jnp.arange(WINDOW)[None, :] == 0, (1 << 21) * WINDOW, 0)
    unused, picked = lax.top_k(scores + forced, K)
    ids = jnp.arange(BLOCKS)[:, None] - 1 - picked
    return jnp.where(ids >= 0, ids, -1).astype(jnp.int32)


def draw_sources(key, part):
    key = jax.random.fold_in(key, 53)
    scores = jax.random.randint(key, (TILES, WINDOW), 0, 1 << 20) * WINDOW + jnp.arange(WINDOW)[None, :]
    forced = jnp.where(jnp.arange(WINDOW)[None, :] == 0, (1 << 21) * WINDOW, 0)
    unused, picked = lax.top_k(scores + forced, KP)
    last = jnp.arange(TILES) // TP * NB + NB - 1
    ids = last[:, None] - picked
    return jnp.where(ids >= 0, ids, -1).astype(jnp.int32)


def draw_theta(key, part):
    key = jax.random.fold_in(key, 67)
    lower = jnp.array([0.8, 0.15, 0.25, 0.1, 0.05, 0.8], jnp.float32)
    upper = jnp.array([1.6, 0.4, 0.5, 0.4, 0.2, 1.25], jnp.float32)
    return lower + (upper - lower) * jax.random.uniform(key, (6,), jnp.float32)


def levels(stream_key, dims, pieces, least, top_value):
    loudness, own = 1.0, jax.random.fold_in(stream_key, 6)
    for axis_at, parts in pieces:
        steps = jnp.exp(jax.random.uniform(jax.random.fold_in(own, axis_at), (parts,), jnp.float32, least / len(pieces), top_value / len(pieces)))
        loudness = loudness * jnp.repeat(steps, dims[axis_at] // parts).reshape([-1 if axis == axis_at else 1 for axis in range(len(dims))])
    return loudness


def centred(rng, shape, deviation, limit, pieces=(), held_as=jnp.bfloat16):
    drawn = deviation * jax.random.normal(rng, shape, jnp.float32)
    if pieces:
        drawn = drawn * levels(rng, shape, pieces, -0.22, 0.18)
    return jnp.clip(drawn, -limit, limit).astype(held_as)


def setup_inputs(seed: int = 0) -> dict:
    splits = jax.random.split(jax.random.key(seed), 8)
    coords = draw_coords(jax.random.fold_in(splits[7], 71), 0)
    values = centred(splits[1], (BLOCKS, R, BS), 1.0, 6.0, ((0, 32),), jnp.float32)
    valid = draw_valid(jax.random.fold_in(splits[7], 71), 0)
    neighbours = draw_neighbours(jax.random.fold_in(splits[7], 71), 0)
    grid = draw_grid(jax.random.fold_in(splits[7], 71), 0)
    sources = draw_sources(jax.random.fold_in(splits[7], 71), 0)
    theta = draw_theta(jax.random.fold_in(splits[7], 71), 0)
    return {"coords": coords, "values": values, "valid": valid, "neighbours": neighbours, "grid": grid, "sources": sources, "theta": theta}


def lower_solve(factor, rhs):
    return lax.linalg.triangular_solve(factor, rhs, left_side=True, lower=True)

def site_mask(valid_rows, width):
    return (jnp.arange(width)[None, :] < valid_rows[:, None]).astype(jnp.float32)

def tukey_inverse(data, theta):
    shape_g = theta[3]
    shape_h = theta[4]
    omega = theta[5]
    target = data / omega
    point = jnp.zeros_like(target)
    for step in range(NEWTON):
        grow = jnp.exp(shape_g * point)
        heavy = jnp.exp(0.5 * shape_h * point * point)
        value = (grow - 1.0) / shape_g * heavy
        slope = grow * heavy + shape_h * point * value
        point = point - (value - target) / slope
    grow = jnp.exp(shape_g * point)
    heavy = jnp.exp(0.5 * shape_h * point * point)
    value = (grow - 1.0) / shape_g * heavy
    slope = grow * heavy + shape_h * point * value
    return (point, jnp.log(omega * slope))

def tukey_forward(point, theta):
    return theta[5] * (jnp.exp(theta[3] * point) - 1.0) / theta[3] * jnp.exp(0.5 * theta[4] * point * point)

def covariance(first, second, theta):
    across = first[0][:, None] - second[0][None, :]
    along = first[1][:, None] - second[1][None, :]
    return theta[0] * jnp.exp(-jnp.sqrt(across * across + along * along) / theta[1])

def factor_of(points, weight, theta):
    matrix = covariance(points, points, theta) * weight[:, None] * weight[None, :]
    matrix = matrix + jnp.diag(theta[2] * weight + 1.0 - weight)
    return jnp.linalg.cholesky(matrix)

def collect(ids, coords, latent, masks):
    present = (ids >= 0).astype(jnp.float32)
    safe = jnp.maximum(ids, 0).astype(jnp.int32)
    points = jnp.take(coords, safe, axis=0).transpose(1, 0, 2).reshape(2, -1)
    weight = (jnp.take(masks, safe, axis=0) * present[:, None]).reshape(-1)
    rows = jnp.take(latent, safe, axis=0)
    data = rows.transpose(1, 0, 2).reshape(rows.shape[1], -1) * weight[None, :]
    return (points, weight, data)

def reference(coords, values, valid, neighbours, grid, sources, theta):
    latent, logjac = tukey_inverse(values, theta)
    masks = site_mask(valid, BS)

    def condition(index):
        ids = jnp.concatenate([neighbours[index], index[None]]).astype(jnp.int32)
        points, weight, data = collect(ids, coords, latent, masks)
        factor = factor_of(points, weight, theta)
        white = lower_solve(factor, data.T)
        own_white = white[K * BS:, :].T
        logdiag = jnp.log(jnp.diagonal(factor))[K * BS:]
        term = -0.5 * jnp.sum(own_white * own_white) - R * jnp.sum(logdiag)
        term = term - 0.5 * R * math.log(2.0 * math.pi) * jnp.sum(masks[index])
        term = term - jnp.sum(logjac[index] * masks[index][None, :])
        return (own_white, term)
    whitened, terms = lax.map(condition, jnp.arange(BLOCKS, dtype=jnp.int32))

    def predict(index):
        points, weight, data = collect(sources[index], coords, latent, masks)
        factor = factor_of(points, weight, theta)
        solved = lower_solve(factor, data.T)
        cross = covariance(points, grid[index], theta) * weight[:, None]
        reach = lower_solve(factor, cross)
        mean = jnp.dot(solved.T.astype(jnp.float32), reach.astype(jnp.float32), precision=lax.Precision.HIGHEST, preferred_element_type=jnp.float32)
        return tukey_forward(mean, theta)
    predicted = lax.map(predict, jnp.arange(TILES, dtype=jnp.int32))
    count = jnp.sum(valid.astype(jnp.float32))
    loglik = jnp.sum(terms) / (R * count)
    return (whitened, predicted, loglik)
```

```python
import functools
import math

import jax
import jax.numpy as jnp
from jax import lax
from jax.experimental import pallas as pl
from jax.experimental.pallas import tpu as pltpu
from jax.sharding import PartitionSpec as P

HIST = 2
NEWTON = 8
TILE = 128
GROUP = (8, 128)
ROWS = 40
HI = lax.Precision.HIGHEST


def passed_along(value, axis, steps):
    count = lax.axis_size(axis)
    initial, last = (max(0, -steps), min(count, count - steps))
    return lax.ppermute(value, axis, [(source, source + steps) for source in range(initial, last)])


def summed_over(value, axis):
    count = lax.axis_size(axis)
    if count & (count - 1):
        total = value
        for _ in range(count - 1):
            value = lax.ppermute(value, axis, [(i, (i + 1) % count) for i in range(count)])
            total = total + value
        return total
    step = 1
    while step < count:
        value = value + lax.ppermute(value, axis, [(i, i ^ step) for i in range(count)])
        step *= 2
    return value


def prepare_kernel(values_ref, coords_ref, valid_ref, theta_ref, packed_ref, extra_ref):
    reps, width = values_ref.shape[1], values_ref.shape[2]
    shape_g, shape_h, omega = theta_ref[3], theta_ref[4], theta_ref[5]
    one = jnp.ones((1, width), jnp.float32)
    inv_g = 1.0 / (one * shape_g)
    inv_omega = 1.0 / (one * omega)
    half_h = 0.5 * shape_h

    def parts(point):
        grow = jnp.exp(shape_g * point)
        heavy = jnp.exp(half_h * point * point)
        value = (grow - 1.0) * inv_g * heavy
        return value, grow * heavy + shape_h * point * value

    for index in range(values_ref.shape[0]):
        lane = lax.broadcasted_iota(jnp.int32, (1, width), 1)
        mask = (lane < valid_ref[index]).astype(jnp.float32)
        target = values_ref[index] * inv_omega
        point = jnp.zeros_like(target)
        for _ in range(NEWTON):
            value, slope = parts(point)
            point = point - (value - target) / slope
        _, slope = parts(point)
        logjac = jnp.log(omega * slope) * mask
        packed_ref[index, 0:reps, :] = point * mask
        packed_ref[index, reps : reps + 2, :] = coords_ref[index]
        packed_ref[index, reps + 2 : reps + 3, :] = mask
        packed_ref[index, reps + 3 :, :] = jnp.zeros((ROWS - reps - 3, width), jnp.float32)
        live = jnp.sum(mask)
        part = -jnp.sum(logjac) - 0.5 * reps * math.log(2.0 * math.pi) * live
        at = lax.broadcasted_iota(jnp.int32, GROUP, 1)
        extra_ref[index] = jnp.where(at == 0, part, jnp.where(at == 1, live, 0.0))


def over_sublanes(x, j):
    return jnp.broadcast_to(x[j : j + 1, :], GROUP)


def over_lanes(x, j):
    return jnp.broadcast_to(x[:, j : j + 1], GROUP)


def factor_tile(rows):
    count = len(rows)
    rows = list(rows)
    sub = lax.broadcasted_iota(jnp.int32, GROUP, 0)
    lane = lax.broadcasted_iota(jnp.int32, GROUP, 1)
    inverse = [jnp.where(lane == sub + 8 * q, 1.0, 0.0).astype(jnp.float32) for q in range(count)]
    pivots = []
    diag = [over_lanes(rows[0], j) for j in range(8)]
    for p in range(count):
        cols = {q: [over_lanes(rows[q], 8 * p + j) for j in range(8)] for q in range(p + 1, count)}
        if p + 1 < count:
            ahead = [over_lanes(rows[p + 1], 8 * (p + 1) + j) for j in range(8)]
        recips, upper, own_rows, own_inv = [], {}, [], []
        pivot = jnp.zeros(GROUP, jnp.float32)
        row, inv = rows[p], inverse[p]
        for j in range(8):
            d = over_sublanes(diag[j], j)
            r = 1.0 / d
            recips.append(r)
            pivot = jnp.where(sub == j, d, pivot)
            for k in range(j + 1, 8):
                upper[j, k] = over_sublanes(diag[k], j)
                diag[k] = diag[k] - (diag[j] * upper[j, k]) * r
            own_rows.append(over_sublanes(row, j))
            own_inv.append(over_sublanes(inv, j))
            if j < 7:
                m = jnp.where(sub > j, diag[j] * r, 0.0)
                row = row - m * own_rows[j]
                inv = inv - m * own_inv[j]
        inverse[p] = inv
        pivots.append(pivot)
        for q in range(p + 1, count):
            t, e = rows[q], inverse[q]
            for j in range(8):
                v = cols[q][j]
                f = v * recips[j]
                if q == p + 1:
                    for k in range(8):
                        ahead[k] = ahead[k] - f * over_sublanes(v, k)
                for k in range(j + 1, 8):
                    cols[q][k] = cols[q][k] - f * upper[j, k]
                t = t - f * own_rows[j]
                e = e - f * own_inv[j]
            rows[q], inverse[q] = t, e
        if p + 1 < count:
            diag = ahead
    return [inverse[q] * lax.rsqrt(pivots[q]) for q in range(count)], pivots


def load_set(blocks, window_ref, theta_ref, reps, width, w_ref, xb_ref, yb_ref, mb_ref, data_at):
    s2, rho, nug = theta_ref[0], theta_ref[1], theta_ref[2]
    slope = -1.0 / jnp.full((1, TILE), rho, jnp.float32)
    per = width // TILE
    for n, (index, present) in enumerate(blocks):
        block = window_ref[index]
        full = jnp.concatenate([block, jnp.zeros((TILE - ROWS, width), jnp.float32)], axis=0)
        turned = jnp.transpose(full)
        at = slice(n * width, (n + 1) * width)
        xb_ref[at, :] = jnp.broadcast_to(turned[:, reps : reps + 1], (width, TILE))
        yb_ref[at, :] = jnp.broadcast_to(turned[:, reps + 1 : reps + 2], (width, TILE))
        mb_ref[at, :] = jnp.broadcast_to(turned[:, reps + 2 : reps + 3] * present, (width, TILE))
        w_ref[at, data_at : data_at + TILE] = turned * present
    sub = lax.broadcasted_iota(jnp.int32, (TILE, TILE), 0)
    lane = lax.broadcasted_iota(jnp.int32, (TILE, TILE), 1)
    for n, (index, present) in enumerate(blocks):
        for part in range(per):
            c = n * per + part
            lanes = slice(part * TILE, (part + 1) * TILE)
            xr = window_ref[index, reps : reps + 1, lanes]
            yr = window_ref[index, reps + 1 : reps + 2, lanes]
            mr = window_ref[index, reps + 2 : reps + 3, lanes] * present

            def tile(at):
                dx = xb_ref[at, :] - xr
                dy = yb_ref[at, :] - yr
                return jnp.exp(jnp.sqrt(dx * dx + dy * dy) * slope) * (mb_ref[at, :] * (mr * s2))

            for r in range(c):
                at = slice(r * TILE, (r + 1) * TILE)
                w_ref[at, c * TILE : (c + 1) * TILE] = tile(at)
            at = slice(c * TILE, (c + 1) * TILE)
            w_ref[at, at] = jnp.where(sub == lane, mr * (s2 + nug) + (1.0 - mr), tile(at))


def eliminate(count, total, w_ref, li_ref, ld_ref):
    def step(k, carry):
        off = pl.multiple_of(k * TILE, TILE)
        rows = [w_ref[pl.ds(off + 8 * q, 8), pl.ds(off, TILE)] for q in range(TILE // 8)]
        inverse, pivots = factor_tile(rows)
        logs = jnp.zeros(GROUP, jnp.float32)
        for q in range(TILE // 8):
            li_ref[8 * q : 8 * q + 8, :] = inverse[q]
            logs = logs + jnp.log(pivots[q])
        ld_ref[k] = logs
        for kk in range(count):

            @pl.when(k == kk)
            def _():
                at = slice(kk * TILE, (kk + 1) * TILE)
                start = (kk + 1) * TILE
                w_ref[at, start:total] = lax.dot(
                    li_ref[...], w_ref[at, start:total], precision=HI, preferred_element_type=jnp.float32
                )
                for i in range(kk + 1, count):
                    rows_at = slice(i * TILE, (i + 1) * TILE)
                    w_ref[rows_at, i * TILE : total] -= lax.dot_general(
                        w_ref[at, rows_at],
                        w_ref[at, i * TILE : total],
                        (((0,), (0,)), ((), ())),
                        precision=HI,
                        preferred_element_type=jnp.float32,
                    )

        return carry

    lax.fori_loop(0, count, step, 0)


def condition_kernel(
    window_ref, extra_ref, ids_ref, theta_ref, white_ref, term_ref, w_ref, xb_ref, yb_ref, mb_ref, li_ref, ld_ref,
    *, reps, sets,
):
    width = window_ref.shape[2]
    count = sets * width // TILE
    blocks = [(ids_ref[i], (ids_ref[sets + i]).astype(jnp.float32)) for i in range(sets)]
    load_set(blocks, window_ref, theta_ref, reps, width, w_ref, xb_ref, yb_ref, mb_ref, count * TILE)
    eliminate(count, (count + 1) * TILE, w_ref, li_ref, ld_ref)
    own = slice((sets - 1) * width, sets * width)
    white = jnp.transpose(w_ref[own, count * TILE : (count + 1) * TILE])[0:reps, :]
    white_ref[...] = white
    logs = ld_ref[count - width // TILE]
    for i in range(count - width // TILE + 1, count):
        logs = logs + ld_ref[i]
    at = lax.broadcasted_iota(jnp.int32, GROUP, 1)
    logdet = 0.5 * jnp.sum(jnp.where(at == 0, logs, 0.0))
    term = -0.5 * jnp.sum(white * white) - reps * logdet
    term_ref[...] = extra_ref[...] + jnp.where(at == 0, term, 0.0)


def predict_kernel(
    window_ref, grid_ref, ids_ref, theta_ref, out_ref, w_ref, xb_ref, yb_ref, mb_ref, li_ref, ld_ref, *, reps, sets
):
    width = window_ref.shape[2]
    points = grid_ref.shape[1]
    count = sets * width // TILE
    blocks = [(ids_ref[i], (ids_ref[sets + i]).astype(jnp.float32)) for i in range(sets)]
    data_at = count * TILE
    load_set(blocks, window_ref, theta_ref, reps, width, w_ref, xb_ref, yb_ref, mb_ref, data_at)
    s2 = theta_ref[0]
    slope = -1.0 / jnp.full((1, TILE), theta_ref[1], jnp.float32)
    grid_at = data_at + TILE
    for c in range(points // TILE):
        lanes = slice(c * TILE, (c + 1) * TILE)
        xr, yr = grid_ref[0:1, lanes], grid_ref[1:2, lanes]
        for r in range(count):
            at = slice(r * TILE, (r + 1) * TILE)
            dx = xb_ref[at, :] - xr
            dy = yb_ref[at, :] - yr
            w_ref[at, grid_at + c * TILE : grid_at + (c + 1) * TILE] = (
                jnp.exp(jnp.sqrt(dx * dx + dy * dy) * slope) * (mb_ref[at, :] * s2)
            )
    eliminate(count, grid_at + points, w_ref, li_ref, ld_ref)
    mean = lax.dot_general(
        w_ref[:, data_at : data_at + TILE],
        w_ref[:, grid_at : grid_at + points],
        (((0,), (0,)), ((), ())),
        precision=HI,
        preferred_element_type=jnp.float32,
    )[0:reps, :]
    shape_g, half_h = theta_ref[3], 0.5 * theta_ref[4]
    scale = theta_ref[5] / jnp.full((1, points), shape_g, jnp.float32)
    out_ref[...] = scale * (jnp.exp(shape_g * mean) - 1.0) * jnp.exp(half_h * mean * mean)


VMEM = pl.BlockSpec(memory_space=pltpu.VMEM)
SMEM = pl.BlockSpec(memory_space=pltpu.SMEM)


def scratch(sets, width, extra):
    sites = sets * width
    return [
        pltpu.VMEM((sites, sites + extra), jnp.float32),
        pltpu.VMEM((sites, TILE), jnp.float32),
        pltpu.VMEM((sites, TILE), jnp.float32),
        pltpu.VMEM((sites, TILE), jnp.float32),
        pltpu.VMEM((TILE, TILE), jnp.float32),
        pltpu.VMEM((sites // TILE,) + GROUP, jnp.float32),
    ]


PARAMS = pltpu.CompilerParams(vmem_limit_bytes=40 * 1024 * 1024)


def body(coords, values, valid, neighbours, grid, sources, theta):
    blocks, _, width = coords.shape
    reps = values.shape[1]
    tiles, _, points = grid.shape
    n_blk = lax.axis_size("blk")
    group = blocks * n_blk
    space_index = lax.axis_index("space")
    first_id = (space_index * n_blk + lax.axis_index("blk")) * blocks
    base = (space_index - HIST) * group
    packed, extra = pl.pallas_call(
        prepare_kernel,
        out_shape=(
            jax.ShapeDtypeStruct((blocks, ROWS, width), jnp.float32),
            jax.ShapeDtypeStruct((blocks,) + GROUP, jnp.float32),
        ),
        in_specs=[VMEM, VMEM, SMEM, SMEM],
        out_specs=(VMEM, VMEM),
        name="prepare",
    )(values, coords, valid, theta)
    grouped = lax.all_gather(packed, "blk", axis=0, tiled=True)
    pieces = [grouped]
    for step in range(1, HIST + 1):
        pieces.insert(0, passed_along(grouped, "space", step))
    window = jnp.concatenate(pieces, axis=0)

    own_ids = first_id + jnp.arange(blocks, dtype=jnp.int32)[:, None]
    cond_ids = jnp.concatenate([neighbours, own_ids], axis=1)

    def listed(ids):
        present = (ids >= 0).astype(jnp.int32)
        return jnp.concatenate([jnp.where(ids >= 0, ids - base, 0), present], axis=1)

    cond_list, pred_list = listed(cond_ids), listed(sources)
    whitened, terms, predicted = [], [], []
    sets = cond_ids.shape[1]
    for index in range(blocks):
        white, term = pl.pallas_call(
            functools.partial(condition_kernel, reps=reps, sets=sets),
            out_shape=(
                jax.ShapeDtypeStruct((reps, width), jnp.float32),
                jax.ShapeDtypeStruct(GROUP, jnp.float32),
            ),
            in_specs=[VMEM, VMEM, SMEM, SMEM],
            out_specs=(VMEM, VMEM),
            scratch_shapes=scratch(sets, width, TILE),
            compiler_params=PARAMS,
            name="condition",
        )(window, extra[index], cond_list[index], theta)
        whitened.append(white)
        terms.append(term)
    sets = sources.shape[1]
    for index in range(tiles):
        predicted.append(
            pl.pallas_call(
                functools.partial(predict_kernel, reps=reps, sets=sets),
                out_shape=jax.ShapeDtypeStruct((reps, points), jnp.float32),
                in_specs=[VMEM, VMEM, SMEM, SMEM],
                out_specs=VMEM,
                scratch_shapes=scratch(sets, width, TILE + points),
                compiler_params=PARAMS,
                name="predict",
            )(window, grid[index], pred_list[index], theta)
        )
    total = sum(terms[1:], terms[0])[0:1]
    total = summed_over(summed_over(total, "blk"), "space")
    loglik = total[0, 0] / (reps * total[0, 1])
    return jnp.stack(whitened), jnp.stack(predicted), loglik


def solution(mesh):
    rows = P(("space", "blk"), None, None)
    return jax.shard_map(
        body,
        mesh=mesh,
        in_specs=(rows, rows, P(("space", "blk")), P(("space", "blk"), None), rows, P(("space", "blk"), None), P()),
        out_specs=(rows, rows, P()),
        check_vma=False,
    )
```

```python
import functools
import math

import jax
import jax.numpy as jnp
from jax import lax
from jax.experimental import pallas as pl
from jax.experimental.pallas import tpu as pltpu
from jax.sharding import PartitionSpec as P

HIST = 2
NEWTON = 8
TILE = 128
GROUP = (8, 128)
ROWS = 40
HI = lax.Precision.HIGHEST


def passed_along(value, axis, steps):
    count = lax.axis_size(axis)
    initial, last = (max(0, -steps), min(count, count - steps))
    return lax.ppermute(value, axis, [(source, source + steps) for source in range(initial, last)])


def summed_over(value, axis):
    count = lax.axis_size(axis)
    if count & (count - 1):
        total = value
        for _ in range(count - 1):
            value = lax.ppermute(value, axis, [(i, (i + 1) % count) for i in range(count)])
            total = total + value
        return total
    step = 1
    while step < count:
        value = value + lax.ppermute(value, axis, [(i, i ^ step) for i in range(count)])
        step *= 2
    return value


def prepare_kernel(values_ref, coords_ref, valid_ref, theta_ref, packed_ref, extra_ref):
    reps, width = values_ref.shape[1], values_ref.shape[2]
    shape_g, shape_h, omega = theta_ref[3], theta_ref[4], theta_ref[5]
    one = jnp.ones((1, width), jnp.float32)
    inv_g = 1.0 / (one * shape_g)
    inv_omega = 1.0 / (one * omega)
    half_h = 0.5 * shape_h

    def parts(point):
        grow = jnp.exp(shape_g * point)
        heavy = jnp.exp(half_h * point * point)
        value = (grow - 1.0) * inv_g * heavy
        return value, grow * heavy + shape_h * point * value

    for index in range(values_ref.shape[0]):
        lane = lax.broadcasted_iota(jnp.int32, (1, width), 1)
        mask = (lane < valid_ref[index]).astype(jnp.float32)
        target = values_ref[index] * inv_omega
        point = jnp.zeros_like(target)
        for _ in range(NEWTON):
            value, slope = parts(point)
            point = point - (value - target) / slope
        _, slope = parts(point)
        logjac = jnp.log(omega * slope) * mask
        packed_ref[index, 0:reps, :] = point * mask
        packed_ref[index, reps : reps + 2, :] = coords_ref[index]
        packed_ref[index, reps + 2 : reps + 3, :] = mask
        packed_ref[index, reps + 3 :, :] = jnp.zeros((ROWS - reps - 3, width), jnp.float32)
        live = jnp.sum(mask)
        part = -jnp.sum(logjac) - 0.5 * reps * math.log(2.0 * math.pi) * live
        at = lax.broadcasted_iota(jnp.int32, GROUP, 1)
        extra_ref[index] = jnp.where(at == 0, part, jnp.where(at == 1, live, 0.0))


def over_sublanes(x, j):
    return jnp.broadcast_to(x[j : j + 1, :], GROUP)


def over_lanes(x, j):
    return jnp.broadcast_to(x[:, j : j + 1], GROUP)


def tree_sum(terms):
    terms = list(terms)
    while len(terms) > 1:
        odd = [terms[-1]] if len(terms) % 2 else []
        terms = [a + b for a, b in zip(terms[::2], terms[1::2])] + odd
    return terms[0]


def eliminate_groups(rows, out, logs, lo, hi, cols_ref):
    sub = lax.broadcasted_iota(jnp.int32, GROUP, 0)
    lane = lax.broadcasted_iota(jnp.int32, GROUP, 1)
    unit = [jnp.where(sub == j, 1.0, 0.0).astype(jnp.float32) for j in range(8)]

    def extract(p):
        for j in range(8):
            for q in range(p + 1, hi):
                cols_ref[p % 2, (q - lo) * 8 + j] = over_lanes(rows[q], 8 * p + j)

    diag = [over_lanes(rows[lo], 8 * lo + j) for j in range(8)]
    extract(lo)
    yield
    for p in range(lo, hi):
        panel = (lane >= 8 * p) & (lane < 8 * p + 8)
        start = jnp.where(panel, jnp.where(lane == sub + 8 * p, 1.0, 0.0), rows[p])
        solved, product, kept = start, None, []
        for j in range(0, 8, 2):
            x, y = diag[j], diag[j + 1]
            a, b, c = over_sublanes(x, j), over_sublanes(x, j + 1), over_sublanes(y, j + 1)
            det = a * c - b * b
            recip = 1.0 / det
            x, y = x - unit[j], y - unit[j + 1]
            nx, ny = c * x - b * y, a * y - b * x
            for k in range(j + 2, 8):
                u, v = over_sublanes(diag[k], j), over_sublanes(diag[k], j + 1)
                diag[k] = diag[k] - (nx * u + ny * v) * recip
            solved = solved - (nx * over_sublanes(solved, j) + ny * over_sublanes(solved, j + 1)) * recip
            kept.append((a, b, recip, nx, ny))
            product = det if product is None else product * det
            yield
        if p + 1 < hi:
            across = [over_sublanes(solved, j) for j in range(8)]

            def update(q):
                moved = tree_sum([cols_ref[p % 2, (q - lo) * 8 + j] * across[j] for j in range(8)])
                rows[q] = jnp.where(panel, 0.0, rows[q]) - moved

            update(p + 1)
            diag = [over_lanes(rows[p + 1], 8 * (p + 1) + j) for j in range(8)]
            yield
            for q in range(p + 2, hi):
                update(q)
            extract(p + 1)
        lower = start
        scale, fix = jnp.zeros(GROUP, jnp.float32), jnp.zeros(GROUP, jnp.float32)
        for j in range(0, 8, 2):
            a, b, recip, nx, ny = kept[j // 2]
            inv_a = 1.0 / a
            u = over_sublanes(lower, j)
            fix = jnp.where(sub == j + 1, (b * inv_a) * u, fix)
            scale = jnp.where(sub == j, inv_a, jnp.where(sub == j + 1, a * recip, scale))
            if j < 6:
                v = over_sublanes(lower, j + 1)
                lower = lower - jnp.where(sub > j + 1, (nx * u + ny * v) * recip, 0.0)
        out[p] = (lower - fix) * jnp.sqrt(scale)
        logs[p] = jnp.log(product)
        yield


def factor_tile(rows, cols_ref, inverse_ref, logs_ref, part=8):
    count = TILE // 8
    rows, out, logs = list(rows), [None] * count, [None] * count
    lane = lax.broadcasted_iota(jnp.int32, GROUP, 1)
    for lo in range(0, count, part):
        hi = lo + part
        yield from eliminate_groups(rows, out, logs, lo, hi, cols_ref)
        for q in range(lo, hi):
            inverse_ref[8 * q : 8 * q + 8, :] = jnp.where(lane < 8 * q + 8, out[q], 0.0)
        if hi < count:
            top = [jnp.where((lane < 8 * q + 8) | (lane >= 8 * hi), out[q], 0.0) for q in range(lo, hi)]
            top = jnp.concatenate(top, axis=0)
            moved = lax.dot_general(
                top[:, 8 * hi :], top, (((0,), (0,)), ((), ())), precision=HI, preferred_element_type=jnp.float32
            )
            done = (lane >= 8 * lo) & (lane < 8 * hi)
            for q in range(hi, count):
                i = 8 * (q - hi)
                rows[q] = jnp.where(done, 0.0, rows[q]) - moved[i : i + 8]
            yield
    logs_ref[...] = tree_sum(logs)


def take_turns(streams, lead):
    for i, stream in enumerate(streams):
        for _ in range(lead * (len(streams) - 1 - i)):
            next(stream, None)
    live = list(streams)
    while live:
        for stream in list(live):
            try:
                next(stream)
            except StopIteration:
                live.remove(stream)


def decay(dx, dy, slope):
    square = jnp.maximum(dx * dx + dy * dy, 1e-30)
    return jnp.exp(square * lax.rsqrt(square) * slope)


def load_set(blocks, window_ref, theta_ref, reps, width, w_ref, xb_ref, yb_ref, mb_ref, data_at):
    s2, rho, nug = theta_ref[0], theta_ref[1], theta_ref[2]
    slope = -1.0 / jnp.full((1, TILE), rho, jnp.float32)
    per = width // TILE
    for n, (index, present) in enumerate(blocks):
        block = window_ref[index]
        full = jnp.concatenate([block, jnp.zeros((TILE - ROWS, width), jnp.float32)], axis=0)
        turned = jnp.transpose(full)
        at = slice(n * width, (n + 1) * width)
        xb_ref[at, :] = jnp.broadcast_to(turned[:, reps : reps + 1], (width, TILE))
        yb_ref[at, :] = jnp.broadcast_to(turned[:, reps + 1 : reps + 2], (width, TILE))
        mb_ref[at, :] = jnp.broadcast_to(turned[:, reps + 2 : reps + 3] * present, (width, TILE))
        w_ref[at, data_at : data_at + TILE] = turned * present
    sub = lax.broadcasted_iota(jnp.int32, (TILE, TILE), 0)
    lane = lax.broadcasted_iota(jnp.int32, (TILE, TILE), 1)
    for n, (index, present) in enumerate(blocks):
        for part in range(per):
            c = n * per + part
            lanes = slice(part * TILE, (part + 1) * TILE)
            xr = window_ref[index, reps : reps + 1, lanes]
            yr = window_ref[index, reps + 1 : reps + 2, lanes]
            mr = window_ref[index, reps + 2 : reps + 3, lanes] * present

            def tile(at):
                dx = xb_ref[at, :] - xr
                dy = yb_ref[at, :] - yr
                return decay(dx, dy, slope) * (mb_ref[at, :] * (mr * s2))

            for r in range(c):
                at = slice(r * TILE, (r + 1) * TILE)
                w_ref[at, c * TILE : (c + 1) * TILE] = tile(at)
            at = slice(c * TILE, (c + 1) * TILE)
            w_ref[at, at] = jnp.where(sub == lane, mr * (s2 + nug) + (1.0 - mr), tile(at))


def thirds(x):
    high = x.astype(jnp.bfloat16)
    rest = x - high.astype(jnp.float32)
    mid = rest.astype(jnp.bfloat16)
    return high, mid, (rest - mid.astype(jnp.float32)).astype(jnp.bfloat16)


def left_parts(x):
    h, m, l = thirds(x)
    return jnp.concatenate([h, h, m, h, l, m], axis=1)


def right_parts(x):
    h, m, l = thirds(x)
    return jnp.concatenate([h, m, h, l, h, m], axis=0)


def product(left, right):
    return lax.dot(left, right, preferred_element_type=jnp.float32)


def eliminate(systems, lo, hi, cols_ref, li_ref):
    def step(k, carry):
        off = pl.multiple_of(k * TILE, TILE)
        streams = []
        for i, (w_ref, logs_ref, _, _) in enumerate(systems):
            rows = [w_ref[pl.ds(off + 8 * q, 8), pl.ds(off, TILE)] for q in range(TILE // 8)]
            streams.append(factor_tile(rows, cols_ref.at[i], li_ref.at[i], logs_ref.at[k]))
        take_turns(streams, 3)
        for kk in range(lo, hi):

            @pl.when(k == kk)
            def _():
                at = slice(kk * TILE, (kk + 1) * TILE)
                start = (kk + 1) * TILE
                rights, lefts = [], []
                for i, (w_ref, _, tiles, total) in enumerate(systems):
                    solved = product(left_parts(li_ref[i]), right_parts(w_ref[at, start:total]))
                    w_ref[at, start:total] = solved
                    if kk + 1 < tiles:
                        rights.append(right_parts(solved))
                        lefts.append(left_parts(jnp.transpose(solved[:, : tiles * TILE - start])))
                row = kk + 1
                while row < max(system[2] for system in systems):
                    end = row + 2 - row % 2
                    for i, (w_ref, _, tiles, total) in enumerate(systems):
                        if row < tiles:
                            first, last = row * TILE, end * TILE
                            w_ref[first:last, first:total] -= product(
                                lefts[i][first - start : last - start], rights[i][:, first - start :]
                            )
                    row = end

        return carry

    lax.fori_loop(lo, hi, step, 0)


def both_kernel(
    window_ref, extra_ref, cond_ref, pred_ref, grid_ref, theta_ref, white_ref, term_ref, out_ref,
    wc_ref, wp_ref, xb_ref, yb_ref, mb_ref, cols_ref, li_ref, lc_ref, lp_ref, *, reps, sets, sources,
):
    width, points = window_ref.shape[2], grid_ref.shape[1]

    def listed(ref, number):
        return [(ref[i], ref[number + i].astype(jnp.float32)) for i in range(number)]

    count, data_at = sources * width // TILE, sources * width
    load_set(listed(pred_ref, sources), window_ref, theta_ref, reps, width, wp_ref, xb_ref, yb_ref, mb_ref, data_at)
    slope = -1.0 / jnp.full((1, TILE), theta_ref[1], jnp.float32)
    grid_at = data_at + TILE
    for c in range(points // TILE):
        lanes = slice(c * TILE, (c + 1) * TILE)
        xr, yr = grid_ref[0:1, lanes], grid_ref[1:2, lanes]
        for r in range(count):
            at = slice(r * TILE, (r + 1) * TILE)
            dx = xb_ref[at, :] - xr
            dy = yb_ref[at, :] - yr
            wp_ref[at, grid_at + c * TILE : grid_at + (c + 1) * TILE] = (
                decay(dx, dy, slope) * (mb_ref[at, :] * theta_ref[0])
            )
    predicting = (wp_ref, lp_ref, count, grid_at + points)
    count, data_at = sets * width // TILE, sets * width
    load_set(listed(cond_ref, sets), window_ref, theta_ref, reps, width, wc_ref, xb_ref, yb_ref, mb_ref, data_at)
    conditioning = (wc_ref, lc_ref, count, data_at + TILE)
    both = min(predicting[2], count)
    eliminate([conditioning, predicting], 0, both, cols_ref, li_ref)
    for system in (conditioning, predicting):
        if system[2] > both:
            eliminate([system], both, system[2], cols_ref, li_ref)

    own = slice((sets - 1) * width, sets * width)
    white = jnp.transpose(wc_ref[own, data_at : data_at + TILE])[0:reps, :]
    white_ref[...] = white
    logs = tree_sum([lc_ref[i] for i in range(count - width // TILE, count)])
    at = lax.broadcasted_iota(jnp.int32, GROUP, 1)
    sub = lax.broadcasted_iota(jnp.int32, GROUP, 0)
    logdet = 0.5 * jnp.sum(jnp.where((at == 0) & (sub == 0), logs, 0.0))
    term = -0.5 * jnp.sum(white * white) - reps * logdet
    term_ref[...] = extra_ref[...] + jnp.where(at == 0, term, 0.0)

    mean = lax.dot_general(
        wp_ref[:, sources * width : sources * width + TILE],
        wp_ref[:, grid_at : grid_at + points],
        (((0,), (0,)), ((), ())),
        precision=HI,
        preferred_element_type=jnp.float32,
    )[0:reps, :]
    shape_g, half_h = theta_ref[3], 0.5 * theta_ref[4]
    scale = theta_ref[5] / jnp.full((1, points), shape_g, jnp.float32)
    out_ref[...] = scale * (jnp.exp(shape_g * mean) - 1.0) * jnp.exp(half_h * mean * mean)


VMEM = pl.BlockSpec(memory_space=pltpu.VMEM)
SMEM = pl.BlockSpec(memory_space=pltpu.SMEM)


PARAMS = pltpu.CompilerParams(vmem_limit_bytes=40 * 1024 * 1024)


def body(coords, values, valid, neighbours, grid, sources, theta):
    blocks, _, width = coords.shape
    reps = values.shape[1]
    tiles, _, points = grid.shape
    n_blk = lax.axis_size("blk")
    group = blocks * n_blk
    space_index = lax.axis_index("space")
    first_id = (space_index * n_blk + lax.axis_index("blk")) * blocks
    base = (space_index - HIST) * group
    packed, extra = pl.pallas_call(
        prepare_kernel,
        out_shape=(
            jax.ShapeDtypeStruct((blocks, ROWS, width), jnp.float32),
            jax.ShapeDtypeStruct((blocks,) + GROUP, jnp.float32),
        ),
        in_specs=[VMEM, VMEM, SMEM, SMEM],
        out_specs=(VMEM, VMEM),
        name="prepare",
    )(values, coords, valid, theta)
    grouped = lax.all_gather(packed, "blk", axis=0, tiled=True)
    pieces = [grouped]
    for step in range(1, HIST + 1):
        pieces.insert(0, passed_along(grouped, "space", step))
    window = jnp.concatenate(pieces, axis=0)

    own_ids = first_id + jnp.arange(blocks, dtype=jnp.int32)[:, None]
    cond_ids = jnp.concatenate([neighbours, own_ids], axis=1)

    def listed(ids):
        present = (ids >= 0).astype(jnp.int32)
        return jnp.concatenate([jnp.where(ids >= 0, ids - base, 0), present], axis=1)

    cond_list, pred_list = listed(cond_ids), listed(sources)
    sets, listed_sources = cond_ids.shape[1], sources.shape[1]
    whitened, terms, predicted = [], [], []
    sites, near = sets * width, listed_sources * width
    wide = max(sites, near)
    for index in range(blocks):
        white, term, field = pl.pallas_call(
            functools.partial(both_kernel, reps=reps, sets=sets, sources=listed_sources),
            out_shape=(
                jax.ShapeDtypeStruct((reps, width), jnp.float32),
                jax.ShapeDtypeStruct(GROUP, jnp.float32),
                jax.ShapeDtypeStruct((reps, points), jnp.float32),
            ),
            in_specs=[VMEM, VMEM, SMEM, SMEM, VMEM, SMEM],
            out_specs=(VMEM, VMEM, VMEM),
            scratch_shapes=[
                pltpu.VMEM((sites, sites + TILE), jnp.float32),
                pltpu.VMEM((near, near + TILE + points), jnp.float32),
                pltpu.VMEM((wide, TILE), jnp.float32),
                pltpu.VMEM((wide, TILE), jnp.float32),
                pltpu.VMEM((wide, TILE), jnp.float32),
                pltpu.VMEM((2, 2, TILE) + GROUP, jnp.float32),
                pltpu.VMEM((2, TILE, TILE), jnp.float32),
                pltpu.VMEM((sites // TILE,) + GROUP, jnp.float32),
                pltpu.VMEM((near // TILE,) + GROUP, jnp.float32),
            ],
            compiler_params=PARAMS,
            name="both",
        )(window, extra[index], cond_list[index], pred_list[index], grid[index], theta)
        whitened.append(white)
        terms.append(term)
        predicted.append(field)
    total = sum(terms[1:], terms[0])[0:1]
    total = summed_over(summed_over(total, "blk"), "space")
    loglik = total[0, 0] / (reps * total[0, 1])
    return jnp.stack(whitened), jnp.stack(predicted), loglik


def solution(mesh):
    rows = P(("space", "blk"), None, None)
    return jax.shard_map(
        body,
        mesh=mesh,
        in_specs=(rows, rows, P(("space", "blk")), P(("space", "blk"), None), rows, P(("space", "blk"), None), P()),
        out_specs=(rows, rows, P()),
        check_vma=False,
    )
```

```python
import functools
import math

import jax
import jax.numpy as jnp
from jax import lax
from jax.experimental import pallas as pl
from jax.experimental.pallas import tpu as pltpu
from jax.sharding import PartitionSpec as P

HIST = 2
NEWTON = 8
TILE = 128
GROUP = (8, 128)
ROWS = 40
HI = lax.Precision.HIGHEST


def passed_along(value, axis, steps):
    count = lax.axis_size(axis)
    initial, last = (max(0, -steps), min(count, count - steps))
    return lax.ppermute(value, axis, [(source, source + steps) for source in range(initial, last)])


def prepare_kernel(values_ref, coords_ref, valid_ref, theta_ref, packed_ref, extra_ref):
    reps, width = values_ref.shape[1], values_ref.shape[2]
    shape_g, shape_h, omega = theta_ref[3], theta_ref[4], theta_ref[5]
    one = jnp.ones((1, width), jnp.float32)
    inv_g = 1.0 / (one * shape_g)
    inv_omega = 1.0 / (one * omega)
    half_h = 0.5 * shape_h

    def parts(point):
        grow = jnp.exp(shape_g * point)
        heavy = jnp.exp(half_h * point * point)
        value = (grow - 1.0) * inv_g * heavy
        return value, grow * heavy + shape_h * point * value

    for index in range(values_ref.shape[0]):
        lane = lax.broadcasted_iota(jnp.int32, (1, width), 1)
        mask = (lane < valid_ref[index]).astype(jnp.float32)
        target = values_ref[index] * inv_omega
        point = jnp.zeros_like(target)
        for _ in range(NEWTON):
            value, slope = parts(point)
            point = point - (value - target) / slope
        _, slope = parts(point)
        logjac = jnp.log(omega * slope) * mask
        packed_ref[index, 0:reps, :] = point * mask
        packed_ref[index, reps : reps + 2, :] = coords_ref[index]
        packed_ref[index, reps + 2 : reps + 3, :] = mask
        packed_ref[index, reps + 3 :, :] = jnp.zeros((ROWS - reps - 3, width), jnp.float32)
        live = jnp.sum(mask)
        part = -jnp.sum(logjac) - 0.5 * reps * math.log(2.0 * math.pi) * live
        at = lax.broadcasted_iota(jnp.int32, GROUP, 1)
        extra_ref[index] = jnp.where(at == 0, part, jnp.where(at == 1, live, 0.0))


def over_sublanes(x, j):
    return jnp.broadcast_to(x[j : j + 1, :], GROUP)


def over_lanes(x, j):
    return jnp.broadcast_to(x[:, j : j + 1], GROUP)


def tree_sum(terms):
    terms = list(terms)
    while len(terms) > 1:
        odd = [terms[-1]] if len(terms) % 2 else []
        terms = [a + b for a, b in zip(terms[::2], terms[1::2])] + odd
    return terms[0]


def eliminate_groups(rows, out, logs, lo, hi, cols_ref):
    sub = lax.broadcasted_iota(jnp.int32, GROUP, 0)
    lane = lax.broadcasted_iota(jnp.int32, GROUP, 1)
    unit = [jnp.where(sub == j, 1.0, 0.0).astype(jnp.float32) for j in range(8)]

    def extract(p):
        for j in range(8):
            for q in range(p + 1, hi):
                cols_ref[p % 2, (q - lo) * 8 + j] = over_lanes(rows[q], 8 * p + j)

    diag = [over_lanes(rows[lo], 8 * lo + j) for j in range(8)]
    extract(lo)
    ahead = [over_lanes(rows[lo + 1], 8 * (lo + 1) + j) for j in range(8)]
    yield
    for p in range(lo, hi):
        panel = (lane >= 8 * p) & (lane < 8 * p + 8)
        start = jnp.where(panel, jnp.where(lane == sub + 8 * p, 1.0, 0.0), rows[p])
        solved, product, kept = start, None, []
        near = p + 1 < hi
        if near:
            cols = [cols_ref[p % 2, (p + 1 - lo) * 8 + j] for j in range(8)]
        for j in range(0, 8, 2):
            x, y = diag[j], diag[j + 1]
            a, b, c = over_sublanes(x, j), over_sublanes(x, j + 1), over_sublanes(y, j + 1)
            det = a * c - b * b
            recip = 1.0 / det
            x, y = x - unit[j], y - unit[j + 1]
            nx, ny = c * x - b * y, a * y - b * x
            if near:
                s, t = cols[j], cols[j + 1]
                ns, nt = (c * s - b * t) * recip, (a * t - b * s) * recip
            for k in range(j + 2, 8):
                u, v = over_sublanes(diag[k], j), over_sublanes(diag[k], j + 1)
                diag[k] = diag[k] - (nx * u + ny * v) * recip
                if near:
                    cols[k] = cols[k] - (ns * u + nt * v)
            if near:
                for k in range(8):
                    ahead[k] = ahead[k] - (ns * over_sublanes(s, k) + nt * over_sublanes(t, k))
            solved = solved - (nx * over_sublanes(solved, j) + ny * over_sublanes(solved, j + 1)) * recip
            kept.append((a, b, recip, nx, ny))
            product = det if product is None else product * det
            yield
        if p + 1 < hi:
            across = [over_sublanes(solved, j) for j in range(8)]

            def update(q):
                moved = tree_sum([cols_ref[p % 2, (q - lo) * 8 + j] * across[j] for j in range(8)])
                rows[q] = jnp.where(panel, 0.0, rows[q]) - moved

            update(p + 1)
            diag = ahead
            yield
            for q in range(p + 2, hi):
                update(q)
            extract(p + 1)
            if p + 2 < hi:
                ahead = [over_lanes(rows[p + 2], 8 * (p + 2) + j) for j in range(8)]
        lower = start
        scale, fix = jnp.zeros(GROUP, jnp.float32), jnp.zeros(GROUP, jnp.float32)
        for j in range(0, 8, 2):
            a, b, recip, nx, ny = kept[j // 2]
            inv_a = 1.0 / a
            u = over_sublanes(lower, j)
            fix = jnp.where(sub == j + 1, (b * inv_a) * u, fix)
            scale = jnp.where(sub == j, inv_a, jnp.where(sub == j + 1, a * recip, scale))
            if j < 6:
                v = over_sublanes(lower, j + 1)
                lower = lower - jnp.where(sub > j + 1, (nx * u + ny * v) * recip, 0.0)
        out[p] = (lower - fix) * jnp.sqrt(scale)
        logs[p] = jnp.log(product)
        yield


def factor_tile(rows, cols_ref, inverse_ref, logs_ref, part=8):
    count = TILE // 8
    rows, out, logs = list(rows), [None] * count, [None] * count
    lane = lax.broadcasted_iota(jnp.int32, GROUP, 1)
    for lo in range(0, count, part):
        hi = lo + part
        yield from eliminate_groups(rows, out, logs, lo, hi, cols_ref)
        for q in range(lo, hi):
            inverse_ref[8 * q : 8 * q + 8, :] = jnp.where(lane < 8 * q + 8, out[q], 0.0)
        if hi < count:
            top = [jnp.where((lane < 8 * q + 8) | (lane >= 8 * hi), out[q], 0.0) for q in range(lo, hi)]
            top = jnp.concatenate(top, axis=0)
            moved = lax.dot_general(
                top[:, 8 * hi :], top, (((0,), (0,)), ((), ())), precision=HI, preferred_element_type=jnp.float32
            )
            done = (lane >= 8 * lo) & (lane < 8 * hi)
            for q in range(hi, count):
                i = 8 * (q - hi)
                rows[q] = jnp.where(done, 0.0, rows[q]) - moved[i : i + 8]
            yield
    logs_ref[...] = tree_sum(logs)


def take_turns(streams, lead):
    for i, stream in enumerate(streams):
        for _ in range(lead * (len(streams) - 1 - i)):
            next(stream, None)
    live = list(streams)
    while live:
        for stream in list(live):
            try:
                next(stream)
            except StopIteration:
                live.remove(stream)


def decay(dx, dy, slope):
    square = jnp.maximum(dx * dx + dy * dy, 1e-30)
    return jnp.exp(square * lax.rsqrt(square) * slope)


def load_set(blocks, window_ref, theta_ref, reps, width, w_ref, xb_ref, yb_ref, mb_ref, data_at):
    s2, rho, nug = theta_ref[0], theta_ref[1], theta_ref[2]
    slope = -1.0 / jnp.full((1, TILE), rho, jnp.float32)
    per = width // TILE
    for n, (index, present) in enumerate(blocks):
        block = window_ref[index]
        full = jnp.concatenate([block, jnp.zeros((TILE - ROWS, width), jnp.float32)], axis=0)
        turned = jnp.transpose(full)
        at = slice(n * width, (n + 1) * width)
        xb_ref[at, :] = jnp.broadcast_to(turned[:, reps : reps + 1], (width, TILE))
        yb_ref[at, :] = jnp.broadcast_to(turned[:, reps + 1 : reps + 2], (width, TILE))
        mb_ref[at, :] = jnp.broadcast_to(turned[:, reps + 2 : reps + 3] * present, (width, TILE))
        w_ref[at, data_at : data_at + TILE] = turned * present
    sub = lax.broadcasted_iota(jnp.int32, (TILE, TILE), 0)
    lane = lax.broadcasted_iota(jnp.int32, (TILE, TILE), 1)
    for n, (index, present) in enumerate(blocks):
        for part in range(per):
            c = n * per + part
            lanes = slice(part * TILE, (part + 1) * TILE)
            xr = window_ref[index, reps : reps + 1, lanes]
            yr = window_ref[index, reps + 1 : reps + 2, lanes]
            mr = window_ref[index, reps + 2 : reps + 3, lanes] * present

            def tile(at):
                dx = xb_ref[at, :] - xr
                dy = yb_ref[at, :] - yr
                return decay(dx, dy, slope) * (mb_ref[at, :] * (mr * s2))

            for r in range(c):
                at = slice(r * TILE, (r + 1) * TILE)
                w_ref[at, c * TILE : (c + 1) * TILE] = tile(at)
            at = slice(c * TILE, (c + 1) * TILE)
            w_ref[at, at] = jnp.where(sub == lane, mr * (s2 + nug) + (1.0 - mr), tile(at))


def thirds(x):
    high = x.astype(jnp.bfloat16)
    rest = x - high.astype(jnp.float32)
    mid = rest.astype(jnp.bfloat16)
    return high, mid, (rest - mid.astype(jnp.float32)).astype(jnp.bfloat16)


def left_parts(x):
    h, m, l = thirds(x)
    return jnp.concatenate([h, h, m, h, l, m], axis=1)


def right_parts(x):
    h, m, l = thirds(x)
    return jnp.concatenate([h, m, h, l, h, m], axis=0)


def product(left, right):
    return lax.dot(left, right, preferred_element_type=jnp.float32)


def eliminate(systems, lo, hi, cols_ref, li_ref):
    def step(k, carry):
        off = pl.multiple_of(k * TILE, TILE)
        streams = []
        for i, (w_ref, logs_ref, _, _) in enumerate(systems):
            rows = [w_ref[pl.ds(off + 8 * q, 8), pl.ds(off, TILE)] for q in range(TILE // 8)]
            streams.append(factor_tile(rows, cols_ref.at[i], li_ref.at[i], logs_ref.at[k]))
        take_turns(streams, 3)
        for kk in range(lo, hi):

            @pl.when(k == kk)
            def _():
                at = slice(kk * TILE, (kk + 1) * TILE)
                start = (kk + 1) * TILE
                rights, lefts = [], []
                for i, (w_ref, _, tiles, total) in enumerate(systems):
                    solved = product(left_parts(li_ref[i]), right_parts(w_ref[at, start:total]))
                    w_ref[at, start:total] = solved
                    if kk + 1 < tiles:
                        rights.append(right_parts(solved))
                        lefts.append(left_parts(jnp.transpose(solved[:, : tiles * TILE - start])))
                row = kk + 1
                while row < max(system[2] for system in systems):
                    end = row + 2 - row % 2
                    for i, (w_ref, _, tiles, total) in enumerate(systems):
                        if row < tiles:
                            first, last = row * TILE, end * TILE
                            w_ref[first:last, first:total] -= product(
                                lefts[i][first - start : last - start], rights[i][:, first - start :]
                            )
                    row = end

        return carry

    lax.fori_loop(lo, hi, step, 0)


def both_kernel(
    window_ref, extra_ref, cond_ref, pred_ref, grid_ref, theta_ref, white_ref, term_ref, out_ref,
    wc_ref, wp_ref, xb_ref, yb_ref, mb_ref, cols_ref, li_ref, lc_ref, lp_ref, *, reps, sets, sources,
):
    width, points = window_ref.shape[2], grid_ref.shape[1]

    def listed(ref, number):
        return [(ref[i], ref[number + i].astype(jnp.float32)) for i in range(number)]

    count, data_at = sources * width // TILE, sources * width
    load_set(listed(pred_ref, sources), window_ref, theta_ref, reps, width, wp_ref, xb_ref, yb_ref, mb_ref, data_at)
    slope = -1.0 / jnp.full((1, TILE), theta_ref[1], jnp.float32)
    grid_at = data_at + TILE
    for c in range(points // TILE):
        lanes = slice(c * TILE, (c + 1) * TILE)
        xr, yr = grid_ref[0:1, lanes], grid_ref[1:2, lanes]
        for r in range(count):
            at = slice(r * TILE, (r + 1) * TILE)
            dx = xb_ref[at, :] - xr
            dy = yb_ref[at, :] - yr
            wp_ref[at, grid_at + c * TILE : grid_at + (c + 1) * TILE] = (
                decay(dx, dy, slope) * (mb_ref[at, :] * theta_ref[0])
            )
    predicting = (wp_ref, lp_ref, count, grid_at + points)
    count, data_at = sets * width // TILE, sets * width
    load_set(listed(cond_ref, sets), window_ref, theta_ref, reps, width, wc_ref, xb_ref, yb_ref, mb_ref, data_at)
    conditioning = (wc_ref, lc_ref, count, data_at + TILE)
    both = min(predicting[2], count)
    eliminate([conditioning, predicting], 0, both, cols_ref, li_ref)
    for system in (conditioning, predicting):
        if system[2] > both:
            eliminate([system], both, system[2], cols_ref, li_ref)

    own = slice((sets - 1) * width, sets * width)
    white = jnp.transpose(wc_ref[own, data_at : data_at + TILE])[0:reps, :]
    white_ref[...] = white
    logs = tree_sum([lc_ref[i] for i in range(count - width // TILE, count)])
    at = lax.broadcasted_iota(jnp.int32, GROUP, 1)
    sub = lax.broadcasted_iota(jnp.int32, GROUP, 0)
    logdet = 0.5 * jnp.sum(jnp.where((at == 0) & (sub == 0), logs, 0.0))
    term = -0.5 * jnp.sum(white * white) - reps * logdet
    term_ref[...] = extra_ref[...] + jnp.where(at == 0, term, 0.0)

    mean = lax.dot_general(
        wp_ref[:, sources * width : sources * width + TILE],
        wp_ref[:, grid_at : grid_at + points],
        (((0,), (0,)), ((), ())),
        precision=HI,
        preferred_element_type=jnp.float32,
    )[0:reps, :]
    shape_g, half_h = theta_ref[3], 0.5 * theta_ref[4]
    scale = theta_ref[5] / jnp.full((1, points), shape_g, jnp.float32)
    out_ref[...] = scale * (jnp.exp(shape_g * mean) - 1.0) * jnp.exp(half_h * mean * mean)


VMEM = pl.BlockSpec(memory_space=pltpu.VMEM)
SMEM = pl.BlockSpec(memory_space=pltpu.SMEM)


PARAMS = pltpu.CompilerParams(vmem_limit_bytes=40 * 1024 * 1024)


def body(coords, values, valid, neighbours, grid, sources, theta):
    blocks, _, width = coords.shape
    reps = values.shape[1]
    tiles, _, points = grid.shape
    n_blk = lax.axis_size("blk")
    group = blocks * n_blk
    space_index = lax.axis_index("space")
    first_id = (space_index * n_blk + lax.axis_index("blk")) * blocks
    base = (space_index - HIST) * group
    packed, extra = pl.pallas_call(
        prepare_kernel,
        out_shape=(
            jax.ShapeDtypeStruct((blocks, ROWS, width), jnp.float32),
            jax.ShapeDtypeStruct((blocks,) + GROUP, jnp.float32),
        ),
        in_specs=[VMEM, VMEM, SMEM, SMEM],
        out_specs=(VMEM, VMEM),
        name="prepare",
    )(values, coords, valid, theta)
    grouped = lax.all_gather(packed, "blk", axis=0, tiled=True)
    pieces = [grouped]
    for step in range(1, HIST + 1):
        pieces.insert(0, passed_along(grouped, "space", step))
    window = jnp.concatenate(pieces, axis=0)

    own_ids = first_id + jnp.arange(blocks, dtype=jnp.int32)[:, None]
    cond_ids = jnp.concatenate([neighbours, own_ids], axis=1)

    def listed(ids):
        present = (ids >= 0).astype(jnp.int32)
        return jnp.concatenate([jnp.where(ids >= 0, ids - base, 0), present], axis=1)

    cond_list, pred_list = listed(cond_ids), listed(sources)
    sets, listed_sources = cond_ids.shape[1], sources.shape[1]
    whitened, terms, predicted = [], [], []
    sites, near = sets * width, listed_sources * width
    wide = max(sites, near)
    for index in range(blocks):
        white, term, field = pl.pallas_call(
            functools.partial(both_kernel, reps=reps, sets=sets, sources=listed_sources),
            out_shape=(
                jax.ShapeDtypeStruct((reps, width), jnp.float32),
                jax.ShapeDtypeStruct(GROUP, jnp.float32),
                jax.ShapeDtypeStruct((reps, points), jnp.float32),
            ),
            in_specs=[VMEM, VMEM, SMEM, SMEM, VMEM, SMEM],
            out_specs=(VMEM, VMEM, VMEM),
            scratch_shapes=[
                pltpu.VMEM((sites, sites + TILE), jnp.float32),
                pltpu.VMEM((near, near + TILE + points), jnp.float32),
                pltpu.VMEM((wide, TILE), jnp.float32),
                pltpu.VMEM((wide, TILE), jnp.float32),
                pltpu.VMEM((wide, TILE), jnp.float32),
                pltpu.VMEM((2, 2, TILE) + GROUP, jnp.float32),
                pltpu.VMEM((2, TILE, TILE), jnp.float32),
                pltpu.VMEM((sites // TILE,) + GROUP, jnp.float32),
                pltpu.VMEM((near // TILE,) + GROUP, jnp.float32),
            ],
            compiler_params=PARAMS,
            name="both",
        )(window, extra[index], cond_list[index], pred_list[index], grid[index], theta)
        whitened.append(white)
        terms.append(term)
        predicted.append(field)
    devices = lax.axis_size("space") * n_blk
    total = jnp.broadcast_to(sum(terms[1:], terms[0])[0:1], (devices, 1, TILE))
    total = jnp.sum(lax.all_to_all(total, ("space", "blk"), 0, 0, tiled=True), axis=0)
    loglik = total[0, 0] / (reps * total[0, 1])
    return jnp.stack(whitened), jnp.stack(predicted), loglik


def solution(mesh):
    rows = P(("space", "blk"), None, None)
    return jax.shard_map(
        body,
        mesh=mesh,
        in_specs=(rows, rows, P(("space", "blk")), P(("space", "blk"), None), rows, P(("space", "blk"), None), P()),
        out_specs=(rows, rows, P()),
        check_vma=False,
    )
```

```python
import functools
import math

import jax
import jax.numpy as jnp
from jax import lax
from jax.experimental import pallas as pl
from jax.experimental.pallas import tpu as pltpu
from jax.sharding import PartitionSpec as P

HIST = 2
NEWTON = 8
TILE = 128
GROUP = (8, 128)
ROWS = 40
HI = lax.Precision.HIGHEST


def passed_along(value, axis, steps):
    count = lax.axis_size(axis)
    initial, last = (max(0, -steps), min(count, count - steps))
    return lax.ppermute(value, axis, [(source, source + steps) for source in range(initial, last)])


def prepare_kernel(values_ref, coords_ref, valid_ref, theta_ref, packed_ref, extra_ref):
    reps, width = values_ref.shape[1], values_ref.shape[2]
    shape_g, shape_h, omega = theta_ref[3], theta_ref[4], theta_ref[5]
    one = jnp.ones((1, width), jnp.float32)
    inv_g = 1.0 / (one * shape_g)
    inv_omega = 1.0 / (one * omega)
    half_h = 0.5 * shape_h

    def parts(point):
        grow = jnp.exp(shape_g * point)
        heavy = jnp.exp(half_h * point * point)
        value = (grow - 1.0) * inv_g * heavy
        return value, grow * heavy + shape_h * point * value

    for index in range(values_ref.shape[0]):
        lane = lax.broadcasted_iota(jnp.int32, (1, width), 1)
        mask = (lane < valid_ref[index]).astype(jnp.float32)
        target = values_ref[index] * inv_omega
        point = jnp.zeros_like(target)
        for _ in range(NEWTON):
            value, slope = parts(point)
            point = point - (value - target) / slope
        _, slope = parts(point)
        logjac = jnp.log(omega * slope) * mask
        packed_ref[index, 0:reps, :] = point * mask
        packed_ref[index, reps : reps + 2, :] = coords_ref[index]
        packed_ref[index, reps + 2 : reps + 3, :] = mask
        packed_ref[index, reps + 3 :, :] = jnp.zeros((ROWS - reps - 3, width), jnp.float32)
        live = jnp.sum(mask)
        part = -jnp.sum(logjac) - 0.5 * reps * math.log(2.0 * math.pi) * live
        at = lax.broadcasted_iota(jnp.int32, GROUP, 1)
        extra_ref[index] = jnp.where(at == 0, part, jnp.where(at == 1, live, 0.0))


def over_sublanes(x, j):
    return jnp.broadcast_to(x[j : j + 1, :], GROUP)


def over_lanes(x, j):
    return jnp.broadcast_to(x[:, j : j + 1], GROUP)


def tree_sum(terms):
    terms = list(terms)
    while len(terms) > 1:
        odd = [terms[-1]] if len(terms) % 2 else []
        terms = [a + b for a, b in zip(terms[::2], terms[1::2])] + odd
    return terms[0]


def eliminate_groups(rows, out, logs, lo, hi, cols_ref):
    sub = lax.broadcasted_iota(jnp.int32, GROUP, 0)
    lane = lax.broadcasted_iota(jnp.int32, GROUP, 1)
    unit = [jnp.where(sub == j, 1.0, 0.0).astype(jnp.float32) for j in range(8)]

    def extract(p):
        for j in range(8):
            for q in range(p + 1, hi):
                cols_ref[p % 2, (q - lo) * 8 + j] = over_lanes(rows[q], 8 * p + j)

    diag = [over_lanes(rows[lo], 8 * lo + j) for j in range(8)]
    extract(lo)
    ahead = [over_lanes(rows[lo + 1], 8 * (lo + 1) + j) for j in range(8)]
    yield
    for p in range(lo, hi):
        panel = (lane >= 8 * p) & (lane < 8 * p + 8)
        start = jnp.where(panel, jnp.where(lane == sub + 8 * p, 1.0, 0.0), rows[p])
        solved, product, kept = start, None, []
        near = p + 1 < hi
        if near:
            cols = [cols_ref[p % 2, (p + 1 - lo) * 8 + j] for j in range(8)]
        for j in range(0, 8, 2):
            x, y = diag[j], diag[j + 1]
            a, b, c = over_sublanes(x, j), over_sublanes(x, j + 1), over_sublanes(y, j + 1)
            det = a * c - b * b
            recip = 1.0 / det
            x, y = x - unit[j], y - unit[j + 1]
            nx, ny = c * x - b * y, a * y - b * x
            if near:
                s, t = cols[j], cols[j + 1]
                ns, nt = (c * s - b * t) * recip, (a * t - b * s) * recip
            for k in range(j + 2, 8):
                u, v = over_sublanes(diag[k], j), over_sublanes(diag[k], j + 1)
                diag[k] = diag[k] - (nx * u + ny * v) * recip
                if near:
                    cols[k] = cols[k] - (ns * u + nt * v)
            if near:
                for k in range(8):
                    ahead[k] = ahead[k] - (ns * over_sublanes(s, k) + nt * over_sublanes(t, k))
            solved = solved - (nx * over_sublanes(solved, j) + ny * over_sublanes(solved, j + 1)) * recip
            kept.append((a, b, recip, nx, ny))
            product = det if product is None else product * det
            yield
        if p + 1 < hi:
            across = [over_sublanes(solved, j) for j in range(8)]

            def update(q):
                moved = tree_sum([cols_ref[p % 2, (q - lo) * 8 + j] * across[j] for j in range(8)])
                rows[q] = jnp.where(panel, 0.0, rows[q]) - moved

            update(p + 1)
            diag = ahead
            yield
            for q in range(p + 2, hi):
                update(q)
            extract(p + 1)
            if p + 2 < hi:
                ahead = [over_lanes(rows[p + 2], 8 * (p + 2) + j) for j in range(8)]
        lower = start
        scale, fix = jnp.zeros(GROUP, jnp.float32), jnp.zeros(GROUP, jnp.float32)
        for j in range(0, 8, 2):
            a, b, recip, nx, ny = kept[j // 2]
            inv_a = 1.0 / a
            u = over_sublanes(lower, j)
            fix = jnp.where(sub == j + 1, (b * inv_a) * u, fix)
            scale = jnp.where(sub == j, inv_a, jnp.where(sub == j + 1, a * recip, scale))
            if j < 6:
                v = over_sublanes(lower, j + 1)
                lower = lower - jnp.where(sub > j + 1, (nx * u + ny * v) * recip, 0.0)
        out[p] = (lower - fix) * jnp.sqrt(scale)
        logs[p] = jnp.log(product)
        yield


def factor_tile(rows, cols_ref, inverse_ref, logs_ref, part=8):
    count = TILE // 8
    rows, out, logs = list(rows), [None] * count, [None] * count
    lane = lax.broadcasted_iota(jnp.int32, GROUP, 1)
    for lo in range(0, count, part):
        hi = lo + part
        yield from eliminate_groups(rows, out, logs, lo, hi, cols_ref)
        for q in range(lo, hi):
            inverse_ref[8 * q : 8 * q + 8, :] = jnp.where(lane < 8 * q + 8, out[q], 0.0)
        if hi < count:
            top = [jnp.where((lane < 8 * q + 8) | (lane >= 8 * hi), out[q], 0.0) for q in range(lo, hi)]
            top = jnp.concatenate(top, axis=0)
            moved = lax.dot_general(
                top[:, 8 * hi :], top, (((0,), (0,)), ((), ())), precision=HI, preferred_element_type=jnp.float32
            )
            done = (lane >= 8 * lo) & (lane < 8 * hi)
            for q in range(hi, count):
                i = 8 * (q - hi)
                rows[q] = jnp.where(done, 0.0, rows[q]) - moved[i : i + 8]
            yield
    logs_ref[...] = tree_sum(logs)


def take_turns(streams):
    live = [[0.0, i, stream, weight] for i, (stream, weight) in enumerate(streams)]
    while live:
        entry = min(live)
        try:
            next(entry[2])
            entry[0] += 1.0 / entry[3]
        except StopIteration:
            live.remove(entry)


def decay(dx, dy, slope):
    square = jnp.maximum(dx * dx + dy * dy, 1e-30)
    return jnp.exp(square * lax.rsqrt(square) * slope)


def load_set(blocks, window_ref, theta_ref, reps, width, w_ref, xb_ref, yb_ref, mb_ref, data_at):
    s2, rho, nug = theta_ref[0], theta_ref[1], theta_ref[2]
    slope = -1.0 / jnp.full((1, TILE), rho, jnp.float32)
    per = width // TILE
    for n, (index, present) in enumerate(blocks):
        block = window_ref[index]
        full = jnp.concatenate([block, jnp.zeros((TILE - ROWS, width), jnp.float32)], axis=0)
        turned = jnp.transpose(full)
        at = slice(n * width, (n + 1) * width)
        xb_ref[at, :] = jnp.broadcast_to(turned[:, reps : reps + 1], (width, TILE))
        yb_ref[at, :] = jnp.broadcast_to(turned[:, reps + 1 : reps + 2], (width, TILE))
        mb_ref[at, :] = jnp.broadcast_to(turned[:, reps + 2 : reps + 3] * present, (width, TILE))
        w_ref[at, data_at : data_at + TILE] = turned * present
    sub = lax.broadcasted_iota(jnp.int32, (TILE, TILE), 0)
    lane = lax.broadcasted_iota(jnp.int32, (TILE, TILE), 1)
    for n, (index, present) in enumerate(blocks):
        for part in range(per):
            c = n * per + part
            lanes = slice(part * TILE, (part + 1) * TILE)
            xr = window_ref[index, reps : reps + 1, lanes]
            yr = window_ref[index, reps + 1 : reps + 2, lanes]
            mr = window_ref[index, reps + 2 : reps + 3, lanes] * present

            def tile(at):
                dx = xb_ref[at, :] - xr
                dy = yb_ref[at, :] - yr
                return decay(dx, dy, slope) * (mb_ref[at, :] * (mr * s2))

            for r in range(c):
                at = slice(r * TILE, (r + 1) * TILE)
                w_ref[at, c * TILE : (c + 1) * TILE] = tile(at)
            at = slice(c * TILE, (c + 1) * TILE)
            w_ref[at, at] = jnp.where(sub == lane, mr * (s2 + nug) + (1.0 - mr), tile(at))


def thirds(x):
    high = x.astype(jnp.bfloat16)
    rest = x - high.astype(jnp.float32)
    mid = rest.astype(jnp.bfloat16)
    return high, mid, (rest - mid.astype(jnp.float32)).astype(jnp.bfloat16)


def left_parts(x):
    h, m, l = thirds(x)
    return jnp.concatenate([h, h, m, h, l, m], axis=1)


def right_parts(x):
    h, m, l = thirds(x)
    return jnp.concatenate([h, m, h, l, h, m], axis=0)


def product(left, right):
    return lax.dot(left, right, preferred_element_type=jnp.float32)


def eliminate(w_ref, logs_ref, tiles, total, cols_ref, li_ref, left_ref, right_ref):
    sites = tiles * TILE

    def rest(k, inverse, turned):
        at, first = slice(k * TILE, (k + 1) * TILE), (k + 2) * TILE
        chunks, lo = [], first
        while lo < total:
            hi = min(lo + 2 * TILE - lo % (2 * TILE) if lo < sites else lo + 2 * TILE, total)
            if lo < sites:
                hi = min(hi, sites)
            chunks.append(slice(lo, hi))
            lo = hi
        below = slice((k + 1) * TILE, first)
        for chunk in chunks:
            solved = product(inverse, right_parts(w_ref[at, chunk]))
            w_ref[at, chunk] = solved
            if k + 1 < tiles:
                right_ref[:, chunk] = right_parts(solved)
                yield
                w_ref[below, chunk] -= product(turned, right_ref[:, chunk])
                if chunk.start < sites:
                    left_ref[chunk, :] = left_parts(jnp.transpose(solved))
            yield
        for i, rows_at in enumerate(chunks):
            if rows_at.start < sites:
                for chunk in chunks[i:]:
                    w_ref[rows_at, chunk] -= product(left_ref[rows_at, :], right_ref[:, chunk])
                    yield

    pending = iter(())
    for k in range(tiles):
        at = slice(k * TILE, (k + 1) * TILE)
        rows = [w_ref[k * TILE + 8 * q : k * TILE + 8 * q + 8, at] for q in range(TILE // 8)]
        beats = 0
        for _ in factor_tile(rows, cols_ref, li_ref, logs_ref.at[k]):
            beats += 1
            if beats % 3 == 0:
                next(pending, None)
            yield
        for _ in pending:
            yield
        inverse = left_parts(li_ref[...])
        turned = None
        if k + 1 < tiles:
            near = slice((k + 1) * TILE, (k + 2) * TILE)
            solved = product(inverse, right_parts(w_ref[at, near]))
            w_ref[at, near] = solved
            yield
            turned = left_parts(jnp.transpose(solved))
            w_ref[near, near] -= product(turned, right_parts(solved))
            yield
            pending = rest(k, inverse, turned)
        else:
            start = (k + 1) * TILE
            w_ref[at, start:total] = product(inverse, right_parts(w_ref[at, start:total]))


def both_kernel(
    window_ref, extra_ref, cond_ref, pred_ref, grid_ref, theta_ref, white_ref, term_ref, out_ref,
    wc_ref, wp_ref, xb_ref, yb_ref, mb_ref, cols_ref, li_ref, lc_ref, lp_ref,
    left_c_ref, left_p_ref, right_c_ref, right_p_ref, *, reps, sets, sources,
):
    width, points = window_ref.shape[2], grid_ref.shape[1]

    def listed(ref, number):
        return [(ref[i], ref[number + i].astype(jnp.float32)) for i in range(number)]

    count, data_at = sources * width // TILE, sources * width
    load_set(listed(pred_ref, sources), window_ref, theta_ref, reps, width, wp_ref, xb_ref, yb_ref, mb_ref, data_at)
    slope = -1.0 / jnp.full((1, TILE), theta_ref[1], jnp.float32)
    grid_at = data_at + TILE
    for c in range(points // TILE):
        lanes = slice(c * TILE, (c + 1) * TILE)
        xr, yr = grid_ref[0:1, lanes], grid_ref[1:2, lanes]
        for r in range(count):
            at = slice(r * TILE, (r + 1) * TILE)
            dx = xb_ref[at, :] - xr
            dy = yb_ref[at, :] - yr
            wp_ref[at, grid_at + c * TILE : grid_at + (c + 1) * TILE] = (
                decay(dx, dy, slope) * (mb_ref[at, :] * theta_ref[0])
            )
    predicting = (wp_ref, lp_ref, count, grid_at + points)
    count, data_at = sets * width // TILE, sets * width
    load_set(listed(cond_ref, sets), window_ref, theta_ref, reps, width, wc_ref, xb_ref, yb_ref, mb_ref, data_at)
    conditioning = (wc_ref, lc_ref, count, data_at + TILE)
    take_turns(
        [
            (eliminate(*conditioning, cols_ref.at[0], li_ref.at[0], left_c_ref, right_c_ref), conditioning[2]),
            (eliminate(*predicting, cols_ref.at[1], li_ref.at[1], left_p_ref, right_p_ref), predicting[2]),
        ]
    )

    own = slice((sets - 1) * width, sets * width)
    white = jnp.transpose(wc_ref[own, data_at : data_at + TILE])[0:reps, :]
    white_ref[...] = white
    logs = tree_sum([lc_ref[i] for i in range(count - width // TILE, count)])
    at = lax.broadcasted_iota(jnp.int32, GROUP, 1)
    sub = lax.broadcasted_iota(jnp.int32, GROUP, 0)
    logdet = 0.5 * jnp.sum(jnp.where((at == 0) & (sub == 0), logs, 0.0))
    term = -0.5 * jnp.sum(white * white) - reps * logdet
    term_ref[...] = extra_ref[...] + jnp.where(at == 0, term, 0.0)

    mean = lax.dot_general(
        wp_ref[:, sources * width : sources * width + TILE],
        wp_ref[:, grid_at : grid_at + points],
        (((0,), (0,)), ((), ())),
        precision=HI,
        preferred_element_type=jnp.float32,
    )[0:reps, :]
    shape_g, half_h = theta_ref[3], 0.5 * theta_ref[4]
    scale = theta_ref[5] / jnp.full((1, points), shape_g, jnp.float32)
    out_ref[...] = scale * (jnp.exp(shape_g * mean) - 1.0) * jnp.exp(half_h * mean * mean)


VMEM = pl.BlockSpec(memory_space=pltpu.VMEM)
SMEM = pl.BlockSpec(memory_space=pltpu.SMEM)


PARAMS = pltpu.CompilerParams(vmem_limit_bytes=40 * 1024 * 1024)


def body(coords, values, valid, neighbours, grid, sources, theta):
    blocks, _, width = coords.shape
    reps = values.shape[1]
    tiles, _, points = grid.shape
    n_blk = lax.axis_size("blk")
    group = blocks * n_blk
    space_index = lax.axis_index("space")
    first_id = (space_index * n_blk + lax.axis_index("blk")) * blocks
    base = (space_index - HIST) * group
    packed, extra = pl.pallas_call(
        prepare_kernel,
        out_shape=(
            jax.ShapeDtypeStruct((blocks, ROWS, width), jnp.float32),
            jax.ShapeDtypeStruct((blocks,) + GROUP, jnp.float32),
        ),
        in_specs=[VMEM, VMEM, SMEM, SMEM],
        out_specs=(VMEM, VMEM),
        name="prepare",
    )(values, coords, valid, theta)
    grouped = lax.all_gather(packed, "blk", axis=0, tiled=True)
    pieces = [grouped]
    for step in range(1, HIST + 1):
        pieces.insert(0, passed_along(grouped, "space", step))
    window = jnp.concatenate(pieces, axis=0)

    own_ids = first_id + jnp.arange(blocks, dtype=jnp.int32)[:, None]
    cond_ids = jnp.concatenate([neighbours, own_ids], axis=1)

    def listed(ids):
        present = (ids >= 0).astype(jnp.int32)
        return jnp.concatenate([jnp.where(ids >= 0, ids - base, 0), present], axis=1)

    cond_list, pred_list = listed(cond_ids), listed(sources)
    sets, listed_sources = cond_ids.shape[1], sources.shape[1]
    whitened, terms, predicted = [], [], []
    sites, near = sets * width, listed_sources * width
    wide = max(sites, near)
    for index in range(blocks):
        white, term, field = pl.pallas_call(
            functools.partial(both_kernel, reps=reps, sets=sets, sources=listed_sources),
            out_shape=(
                jax.ShapeDtypeStruct((reps, width), jnp.float32),
                jax.ShapeDtypeStruct(GROUP, jnp.float32),
                jax.ShapeDtypeStruct((reps, points), jnp.float32),
            ),
            in_specs=[VMEM, VMEM, SMEM, SMEM, VMEM, SMEM],
            out_specs=(VMEM, VMEM, VMEM),
            scratch_shapes=[
                pltpu.VMEM((sites, sites + TILE), jnp.float32),
                pltpu.VMEM((near, near + TILE + points), jnp.float32),
                pltpu.VMEM((wide, TILE), jnp.float32),
                pltpu.VMEM((wide, TILE), jnp.float32),
                pltpu.VMEM((wide, TILE), jnp.float32),
                pltpu.VMEM((2, 2, TILE) + GROUP, jnp.float32),
                pltpu.VMEM((2, TILE, TILE), jnp.float32),
                pltpu.VMEM((sites // TILE,) + GROUP, jnp.float32),
                pltpu.VMEM((near // TILE,) + GROUP, jnp.float32),
                pltpu.VMEM((sites, 6 * TILE), jnp.bfloat16),
                pltpu.VMEM((near, 6 * TILE), jnp.bfloat16),
                pltpu.VMEM((6 * TILE, sites + TILE), jnp.bfloat16),
                pltpu.VMEM((6 * TILE, near + TILE + points), jnp.bfloat16),
            ],
            compiler_params=PARAMS,
            name="both",
        )(window, extra[index], cond_list[index], pred_list[index], grid[index], theta)
        whitened.append(white)
        terms.append(term)
        predicted.append(field)
    devices = lax.axis_size("space") * n_blk
    total = jnp.broadcast_to(sum(terms[1:], terms[0])[0:1], (devices, 1, TILE))
    total = jnp.sum(lax.all_to_all(total, ("space", "blk"), 0, 0, tiled=True), axis=0)
    loglik = total[0, 0] / (reps * total[0, 1])
    return jnp.stack(whitened), jnp.stack(predicted), loglik


def solution(mesh):
    rows = P(("space", "blk"), None, None)
    return jax.shard_map(
        body,
        mesh=mesh,
        in_specs=(rows, rows, P(("space", "blk")), P(("space", "blk"), None), rows, P(("space", "blk"), None), P()),
        out_specs=(rows, rows, P()),
        check_vma=False,
    )
```
